512 devices in a mesh: blk: 128 (over z, y_lo, x), grp: 4 (over y_hi, core).
Axes of the slice: x: 4, y: 8 (y_hi: 2, y_lo: 4; y = y_hi * 4 + y_lo), z: 8, core: 2. Of those that a mesh axis runs over, the one named last changes fastest.
Arguments:
- photo_vectors: bfloat16 [98304, 1152], P('blk'), may hold values from -1 to 1
- caption_vectors: bfloat16 [98304, 1152], P(('blk', 'grp')), may hold values from -1 to 1
- matching_column: int32 [128, 768], P('blk'), may hold values from 0 to 767, each once within a row
- scale_exponent: float32 [1], replicated, may hold values from 0 to 1.4
- score_intercept: float32 [1], replicated, may hold values from -4 to 0
Outputs:
- image_grad: float32 [98304, 1152], P(('blk', 'grp'))
- text_grad: float32 [98304, 1152], P(('blk', 'grp'))
The draws below stay inside these ranges and needn't reach their ends.
Inputs may be any that keep to these rules, and one draw needn't show every extreme that they name: `matching_column`: each row is an arrangement of 0 .. 767.
All inputs are finite; a program needn't handle non-finite values.
Results may differ from the reference program's by a relative error of at most 0.0024.
Values may be sent and summed in bfloat16 or wider, within the bound.
No kernel may reach another device: no remote copies, remote signals or barrier semaphores. Data moves between devices by JAX's collectives and lax.ppermute only.
A program may use at most 64 MiB of HBM per device.

```python
import jax
import jax.numpy as jnp
from jax import lax

D = 1152
B = 768
STEPS = 2
BLOCKS = 128
IMAGES = 98304


def levels(own_key, extent, cuts, least, high):
    def one(dim, parts):
        steps = jax.random.uniform(jax.random.fold_in(jax.random.fold_in(own_key, 6), dim), (parts,), jnp.float32, least / len(cuts), high / len(cuts))
        return jnp.repeat(jnp.exp(steps), extent[dim] // parts).reshape((-1,) + (1,) * (len(extent) - dim - 1))

    gain = one(*cuts[0])
    for cut in cuts[1:]:
        gain = gain * one(*cut)
    return gain


def noise(rng, extent, spread, reach, cuts=(), kind=jnp.bfloat16):
    array = spread * jax.random.normal(rng, extent, jnp.float32)
    if cuts:
        array = array * levels(rng, extent, cuts, -0.22, 0.18)
    return jnp.clip(array, -reach, reach).astype(kind)


def setup_inputs(seed: int = 0) -> dict:
    key_of = jax.random.split(jax.random.key(seed), 6)
    photo_vectors = noise(key_of[0], (IMAGES, D), 0.1715, 1.0, ((0, 128),))
    caption_vectors = noise(key_of[1], (IMAGES, D), 0.1715, 1.0, ((0, 512),))
    matching_column = jax.vmap(lambda own: jax.random.permutation(own, B))(jax.random.split(key_of[2], BLOCKS)).reshape((BLOCKS, B)).astype(jnp.int32)
    scale_exponent = jnp.clip(jax.random.uniform(key_of[3], (1,), jnp.float32, 0.0, 1.4), 0.0, 1.4)
    score_intercept = jnp.clip(jax.random.uniform(key_of[4], (1,), jnp.float32, -4.0, 0.0), -4.0, 0.0)
    return dict(photo_vectors=photo_vectors, caption_vectors=caption_vectors, matching_column=matching_column, scale_exponent=scale_exponent, score_intercept=score_intercept)


def reference(photo_vectors, caption_vectors, matching_column, scale_exponent, score_intercept):
    image_blocks = photo_vectors.reshape(BLOCKS, B, D)
    text_blocks = caption_vectors.reshape(BLOCKS, B, D)
    score_multiplier = jnp.exp(scale_exponent[0])
    group_displacement = score_intercept[0]
    columns = jnp.arange(B, dtype=jnp.int32)
    image_total = jnp.zeros((BLOCKS, B, D), jnp.float32)
    text_total = jnp.zeros((BLOCKS, B, D), jnp.float32)
    for cycle_step in range(STEPS + 1):
        partner = jnp.roll(text_blocks, cycle_step, axis=0)

        def pair_block(operands, first=(cycle_step == 0)):
            photo_entries, caption_entries, positions = operands
            couple_scores = score_multiplier * jnp.dot(photo_entries, caption_entries.T, preferred_element_type=jnp.float32) + group_displacement
            if first:
                target = jnp.where(positions[:, None] == columns[None, :], jnp.float32(1.0), jnp.float32(-1.0))
            else:
                target = jnp.float32(-1.0)
            couple_weight = (-target * jax.nn.sigmoid(-target * couple_scores)).astype(jnp.bfloat16)
            photo_segment = score_multiplier * jnp.dot(couple_weight, caption_entries, preferred_element_type=jnp.float32)
            caption_segment = score_multiplier * jnp.dot(couple_weight.T, photo_entries, preferred_element_type=jnp.float32)
            return photo_segment, caption_segment

        photo_segment, caption_segment = lax.map(pair_block, (image_blocks, partner, matching_column))
        image_total = image_total + photo_segment
        text_total = text_total + jnp.roll(caption_segment, -cycle_step, axis=0)
    return image_total.reshape(IMAGES, D), text_total.reshape(IMAGES, D)
```

```python
import jax
import jax.numpy as jnp
from jax import lax
from jax.sharding import PartitionSpec as P

BF = jnp.bfloat16
F32 = jnp.float32
AXES = ("blk", "grp")
X, Y = 4, 4


def route(distance):
    blocks, parts = lax.axis_size("blk"), lax.axis_size("grp")
    pairs = []
    for b in range(blocks):
        to = (b + distance) % blocks
        wraps = (b // X) % Y > (to // X) % Y
        for g in range(parts):
            pairs.append((b * parts + g, to * parts + (g ^ 2 if wraps else g)))
    return pairs


def sent(block, distance):
    return lax.ppermute(block, AXES, route(distance))


def returned(block, distance):
    return lax.ppermute(block, AXES, [(j, i) for i, j in route(distance)])


def swapped(block, bit):
    n = lax.axis_size("grp")
    return lax.ppermute(block, "grp", [(i, i ^ bit) for i in range(n)])


def on_device(photo, caption, matching_column, scale_exponent, score_intercept):
    scale = jnp.exp(scale_exponent[0])
    bias = score_intercept[0]
    width = caption.shape[0]
    place = lax.axis_index("grp")

    text1 = sent(caption, 1)

    def ordered(rows):
        parts = [
            lax.dynamic_slice_in_dim(rows, (place ^ bits) * width, width, 0)
            for bits in (3, 1, 2, 0)
        ]
        return jnp.concatenate(parts, 0)

    photo = ordered(photo)
    columns = place * width + lax.iota(jnp.int32, width)
    matched = ordered(matching_column[0])[:, None] == columns[None, :]
    own_target = jnp.where(matched, F32(1.0), F32(-1.0))

    def weight(text, target):
        scores = (
            scale
            * lax.dot_general(
                photo, text, (((1,), (1,)), ((), ())), preferred_element_type=F32
            )
            + bias
        )
        return (-target * jax.nn.sigmoid(-target * scores)).astype(BF)

    def text_term(w):
        return scale * lax.dot_general(
            w, photo, (((0,), (0,)), ((), ())), preferred_element_type=F32
        )

    w0 = weight(caption, own_target)
    going, w0 = lax.optimization_barrier((caption, w0))
    text2 = sent(going, 2)
    text_grad = text_term(w0)
    text1, text_grad = lax.optimization_barrier((text1, text_grad))
    w1 = weight(text1, F32(-1.0))
    term1 = text_term(w1).astype(BF)
    early = jnp.dot(w0, caption, preferred_element_type=F32) + jnp.dot(
        w1, text1, preferred_element_type=F32
    )
    text2, term1, early = lax.optimization_barrier((text2, term1, early))
    w2 = weight(text2, F32(-1.0))

    def image_part(rows):
        return scale * (
            early[rows] + jnp.dot(w2[rows], text2, preferred_element_type=F32)
        )

    give = image_part(slice(0, 2 * width)).astype(BF)
    give, w2, term1 = lax.optimization_barrier((give, w2, term1))
    got = swapped(give, 1)
    back1 = returned(term1, 1)
    keep = image_part(slice(2 * width, 4 * width))
    far = (keep[:width] + got[:width].astype(F32)).astype(BF)
    near = keep[width:] + got[width:].astype(F32)
    other = swapped(far, 2)
    back2 = returned(text_term(w2).astype(BF), 2)

    text_grad = text_grad + back1.astype(F32) + back2.astype(F32)
    text_grad, other = lax.optimization_barrier((text_grad, other))
    image_grad = near + other.astype(F32)
    return image_grad, text_grad


def solution(mesh):
    in_specs = (P("blk", None), P(("blk", "grp"), None), P("blk", None), P(), P())
    out_specs = (P(("blk", "grp"), None), P(("blk", "grp"), None))
    return jax.shard_map(
        on_device, mesh=mesh, in_specs=in_specs, out_specs=out_specs, check_vma=False
    )
```

```python
import jax
import jax.numpy as jnp
from jax import lax
from jax.sharding import PartitionSpec as P

BF = jnp.bfloat16
F32 = jnp.float32
AXES = ("blk", "grp")
X, Y = 4, 4


def route(distance):
    blocks, parts = lax.axis_size("blk"), lax.axis_size("grp")
    pairs = []
    for b in range(blocks):
        to = (b + distance) % blocks
        wraps = (b // X) % Y > (to // X) % Y
        for g in range(parts):
            pairs.append((b * parts + g, to * parts + (g ^ 2 if wraps else g)))
    return pairs


def sent(block, distance):
    return lax.ppermute(block, AXES, route(distance))


def turned(block, distance):
    blocks = lax.axis_size("blk")
    return lax.ppermute(
        block,
        "blk",
        [(b, b // X * X + (b - distance) % X) for b in range(blocks)],
    )


def handed_down(block):
    parts = lax.axis_size("grp")
    crossing = [(i, j) for i, j in route(X) if i // parts % X >= X - 2]
    return lax.ppermute(block, AXES, [(j, i) for i, j in crossing])


def swapped(block, bit):
    n = lax.axis_size("grp")
    return lax.ppermute(block, "grp", [(i, i ^ bit) for i in range(n)])


def on_device(photo, caption, matching_column, scale_exponent, score_intercept):
    scale = jnp.exp(scale_exponent[0])
    bias = score_intercept[0]
    width = caption.shape[0]
    place = lax.axis_index("grp")

    text1 = sent(caption, 1)

    def ordered(rows):
        parts = [
            lax.dynamic_slice_in_dim(rows, (place ^ bits) * width, width, 0)
            for bits in (3, 1, 2, 0)
        ]
        return jnp.concatenate(parts, 0)

    photo = ordered(photo)
    columns = place * width + lax.iota(jnp.int32, width)
    matched = ordered(matching_column[0])[:, None] == columns[None, :]
    own_target = jnp.where(matched, F32(1.0), F32(-1.0))

    def weight(text, target):
        scores = (
            scale
            * lax.dot_general(
                photo, text, (((1,), (1,)), ((), ())), preferred_element_type=F32
            )
            + bias
        )
        return (-target * jax.nn.sigmoid(-target * scores)).astype(BF)

    def text_term(w):
        return scale * lax.dot_general(
            w, photo, (((0,), (0,)), ((), ())), preferred_element_type=F32
        )

    w0 = weight(caption, own_target)
    going, w0 = lax.optimization_barrier((caption, w0))
    text2 = sent(going, 2)
    text_grad = text_term(w0)
    text1, text_grad = lax.optimization_barrier((text1, text_grad))
    w1 = weight(text1, F32(-1.0))
    term1 = text_term(w1).astype(BF)
    early = jnp.dot(w0, caption, preferred_element_type=F32) + jnp.dot(
        w1, text1, preferred_element_type=F32
    )
    text2, term1, early = lax.optimization_barrier((text2, term1, early))
    w2 = weight(text2, F32(-1.0))

    def image_part(rows):
        return scale * (
            early[rows] + jnp.dot(w2[rows], text2, preferred_element_type=F32)
        )

    give = image_part(slice(0, 2 * width)).astype(BF)
    give, w2, term1 = lax.optimization_barrier((give, w2, term1))
    got = swapped(give, 1)
    back1 = turned(term1, 1)
    keep = image_part(slice(2 * width, 4 * width))
    far = (keep[:width] + got[:width].astype(F32)).astype(BF)
    near = keep[width:] + got[width:].astype(F32)
    back2 = turned(text_term(w2).astype(BF), 2)
    other = swapped(far, 2)
    x = lax.axis_index("blk") % X
    back1, back2 = back1.astype(F32), back2.astype(F32)
    down = handed_down(jnp.where(x == X - 1, back1 + back2, back2).astype(BF))
    text_grad = (
        text_grad
        + jnp.where(x == X - 1, F32(0.0), back1)
        + jnp.where(x >= X - 2, F32(0.0), back2)
    )

    image_grad = near + other.astype(F32)
    image_grad, down = lax.optimization_barrier((image_grad, down))
    text_grad = text_grad + down.astype(F32)
    return image_grad, text_grad


def solution(mesh):
    in_specs = (P("blk", None), P(("blk", "grp"), None), P("blk", None), P(), P())
    out_specs = (P(("blk", "grp"), None), P(("blk", "grp"), None))
    return jax.shard_map(
        on_device, mesh=mesh, in_specs=in_specs, out_specs=out_specs, check_vma=False
    )
```

```python
import jax
import jax.numpy as jnp
from jax import lax
from jax.sharding import PartitionSpec as P

BF = jnp.bfloat16
F32 = jnp.float32
AXES = ("blk", "grp")
X, Y = 4, 4


def route(distance):
    blocks, parts = lax.axis_size("blk"), lax.axis_size("grp")
    pairs = []
    for b in range(blocks):
        to = (b + distance) % blocks
        wraps = (b // X) % Y > (to // X) % Y
        for g in range(parts):
            pairs.append((b * parts + g, to * parts + (g ^ 2 if wraps else g)))
    return pairs


def sent(block, distance):
    return lax.ppermute(block, AXES, route(distance))


def back(distance):
    return [(j, i) for i, j in route(distance)]


def across(bit):
    count = lax.axis_size("blk") * lax.axis_size("grp")
    return [(i, i ^ bit) for i in range(count)]


def moved(even, odd, even_pairs, odd_pairs):
    pairs = [p for p in even_pairs if p[0] % 2 == 0]
    pairs += [p for p in odd_pairs if p[0] % 2 == 1]
    payload = jnp.where(lax.axis_index("grp") % 2 == 0, even, odd)
    return lax.ppermute(payload, AXES, pairs)


def on_device(photo, caption, matching_column, scale_exponent, score_intercept):
    scale = jnp.exp(scale_exponent[0])
    bias = score_intercept[0]
    width = caption.shape[0]
    place = lax.axis_index("grp")

    text1 = sent(caption, 1)

    def ordered(rows):
        parts = [
            lax.dynamic_slice_in_dim(rows, (place ^ bits) * width, width, 0)
            for bits in (3, 1, 2, 0)
        ]
        return jnp.concatenate(parts, 0)

    photo = ordered(photo)
    columns = place * width + lax.iota(jnp.int32, width)
    matched = ordered(matching_column[0])[:, None] == columns[None, :]
    own_target = jnp.where(matched, F32(1.0), F32(-1.0))

    def weight(text, target):
        scores = (
            scale
            * lax.dot_general(
                photo, text, (((1,), (1,)), ((), ())), preferred_element_type=F32
            )
            + bias
        )
        return (-target * jax.nn.sigmoid(-target * scores)).astype(BF)

    def text_term(w):
        return scale * lax.dot_general(
            w, photo, (((0,), (0,)), ((), ())), preferred_element_type=F32
        )

    w0 = weight(caption, own_target)
    going, w0 = lax.optimization_barrier((caption, w0))
    text2 = sent(going, 2)
    w1 = weight(text1, F32(-1.0))
    term1 = text_term(w1).astype(BF)
    early = jnp.dot(w0, caption, preferred_element_type=F32) + jnp.dot(
        w1, text1, preferred_element_type=F32
    )
    text2, term1, early = lax.optimization_barrier((text2, term1, early))
    w2 = weight(text2, F32(-1.0))

    def image_part(rows):
        return scale * (
            early[rows] + jnp.dot(w2[rows], text2, preferred_element_type=F32)
        )

    give = image_part(slice(0, 2 * width)).astype(BF)
    give, w2, term1 = lax.optimization_barrier((give, w2, term1))
    got = lax.ppermute(give, AXES, across(1))
    keep = image_part(slice(2 * width, 4 * width))
    far = (keep[:width] + got[:width].astype(F32)).astype(BF)
    near = keep[width:] + got[width:].astype(F32)
    far, w2, term1 = lax.optimization_barrier((far, w2, term1))
    first = moved(far, term1, across(2), back(1))
    term2 = text_term(w2).astype(BF)
    second = moved(term1, term2, back(1), back(2))
    third = moved(term2, far, back(2), across(2))
    w0, term2 = lax.optimization_barrier((w0, term2))
    text_grad = text_term(w0)

    even = place % 2 == 0
    other = jnp.where(even, first, third)
    back1 = jnp.where(even, second, first)
    back2 = jnp.where(even, third, second)
    image_grad = near + other.astype(F32)
    text_grad = text_grad + back1.astype(F32) + back2.astype(F32)
    return image_grad, text_grad


def solution(mesh):
    in_specs = (P("blk", None), P(("blk", "grp"), None), P("blk", None), P(), P())
    out_specs = (P(("blk", "grp"), None), P(("blk", "grp"), None))
    return jax.shard_map(
        on_device, mesh=mesh, in_specs=in_specs, out_specs=out_specs, check_vma=False
    )
```

```python
import jax
import jax.numpy as jnp
from jax import lax
from jax.sharding import PartitionSpec as P

BF = jnp.bfloat16
F32 = jnp.float32
AXES = ("blk", "grp")
X, Y = 4, 4


def route(distance):
    blocks, parts = lax.axis_size("blk"), lax.axis_size("grp")
    pairs = []
    for b in range(blocks):
        to = (b + distance) % blocks
        wraps = (b // X) % Y > (to // X) % Y
        for g in range(parts):
            pairs.append((b * parts + g, to * parts + (g ^ 2 if wraps else g)))
    return pairs


def sent(block, distance):
    return lax.ppermute(block, AXES, route(distance))


def turned(block, distance):
    blocks = lax.axis_size("blk")
    return lax.ppermute(
        block,
        "blk",
        [(b, b // X * X + (b - distance) % X) for b in range(blocks)],
    )


def handed_down(block):
    parts = lax.axis_size("grp")
    crossing = [(i, j) for i, j in route(X) if i // parts % X >= X - 2]
    return lax.ppermute(block, AXES, [(j, i) for i, j in crossing])


def swapped(block, bit):
    n = lax.axis_size("grp")
    return lax.ppermute(block, "grp", [(i, i ^ bit) for i in range(n)])


def on_device(photo, caption, matching_column, scale_exponent, score_intercept):
    scale = jnp.exp(scale_exponent[0])
    bias = score_intercept[0]
    width = caption.shape[0]
    place = lax.axis_index("grp")

    text1 = sent(caption, 1)

    def ordered(rows):
        parts = [
            lax.dynamic_slice_in_dim(rows, (place ^ bits) * width, width, 0)
            for bits in (3, 1, 2, 0)
        ]
        return jnp.concatenate(parts, 0)

    photo = ordered(photo)
    columns = place * width + lax.iota(jnp.int32, width)
    matched = ordered(matching_column[0])[:, None] == columns[None, :]
    own_target = jnp.where(matched, F32(1.0), F32(-1.0))

    def weight(text, target):
        scores = (
            scale
            * lax.dot_general(
                photo, text, (((1,), (1,)), ((), ())), preferred_element_type=F32
            )
            + bias
        )
        return (-target * jax.nn.sigmoid(-target * scores)).astype(BF)

    def text_term(w):
        return scale * lax.dot_general(
            w, photo, (((0,), (0,)), ((), ())), preferred_element_type=F32
        )

    w0 = weight(caption, own_target)
    going, w0 = lax.optimization_barrier((caption, w0))
    text2 = sent(going, 2)
    w1 = weight(text1, F32(-1.0))
    term1 = text_term(w1).astype(BF)
    back1 = turned(term1, 1)
    early = jnp.dot(w0, caption, preferred_element_type=F32) + jnp.dot(
        w1, text1, preferred_element_type=F32
    )
    text2, term1, early = lax.optimization_barrier((text2, term1, early))
    w2 = weight(text2, F32(-1.0))

    def image_part(rows):
        return scale * (
            early[rows] + jnp.dot(w2[rows], text2, preferred_element_type=F32)
        )

    give = image_part(slice(0, 2 * width)).astype(BF)
    give, w2, back1 = lax.optimization_barrier((give, w2, back1))
    got = swapped(give, 1)
    keep = image_part(slice(2 * width, 4 * width))
    far = (keep[:width] + got[:width].astype(F32)).astype(BF)
    near = keep[width:] + got[width:].astype(F32)
    term2 = text_term(w2).astype(BF)
    back2 = turned(term2, 2)
    w0, term2 = lax.optimization_barrier((w0, term2))
    text_grad = text_term(w0)
    other = swapped(far, 2)
    x = lax.axis_index("blk") % X
    back1, back2 = back1.astype(F32), back2.astype(F32)
    down = handed_down(jnp.where(x == X - 1, back1 + back2, back2).astype(BF))
    text_grad = (
        text_grad
        + jnp.where(x == X - 1, F32(0.0), back1)
        + jnp.where(x >= X - 2, F32(0.0), back2)
    )

    image_grad = near + other.astype(F32)
    image_grad, down = lax.optimization_barrier((image_grad, down))
    text_grad = text_grad + down.astype(F32)
    return image_grad, text_grad


def solution(mesh):
    in_specs = (P("blk", None), P(("blk", "grp"), None), P("blk", None), P(), P())
    out_specs = (P(("blk", "grp"), None), P(("blk", "grp"), None))
    return jax.shard_map(
        on_device, mesh=mesh, in_specs=in_specs, out_specs=out_specs, check_vma=False
    )
```

```python
import jax
import jax.numpy as jnp
from jax import lax
from jax.sharding import PartitionSpec as P

BF = jnp.bfloat16
F32 = jnp.float32
AXES = ("blk", "grp")
X, Y = 4, 4


def route(distance):
    blocks, parts = lax.axis_size("blk"), lax.axis_size("grp")
    pairs = []
    for b in range(blocks):
        to = (b + distance) % blocks
        wraps = (b // X) % Y > (to // X) % Y
        for g in range(parts):
            pairs.append((b * parts + g, to * parts + (g ^ 2 if wraps else g)))
    return pairs


def sent(block, distance):
    return lax.ppermute(block, AXES, route(distance))


def turned(block, distance):
    blocks = lax.axis_size("blk")
    return lax.ppermute(
        block,
        "blk",
        [(b, b // X * X + (b - distance) % X) for b in range(blocks)],
    )


def handed_down(block):
    parts = lax.axis_size("grp")
    crossing = [(i, j) for i, j in route(X) if i // parts % X >= X - 2]
    return lax.ppermute(block, AXES, [(j, i) for i, j in crossing])


def swapped(block, bit):
    n = lax.axis_size("grp")
    return lax.ppermute(block, "grp", [(i, i ^ bit) for i in range(n)])


def on_device(photo, caption, matching_column, scale_exponent, score_intercept):
    scale = jnp.exp(scale_exponent[0])
    bias = score_intercept[0]
    width = caption.shape[0]
    place = lax.axis_index("grp")

    text1 = sent(caption, 1)

    def ordered(rows):
        parts = [
            lax.dynamic_slice_in_dim(rows, (place ^ bits) * width, width, 0)
            for bits in (3, 1, 2, 0)
        ]
        return jnp.concatenate(parts, 0)

    photo = ordered(photo)
    columns = place * width + lax.iota(jnp.int32, width)
    matched = ordered(matching_column[0])[:, None] == columns[None, :]
    own_target = jnp.where(matched, F32(1.0), F32(-1.0))

    def weight(text, target):
        scores = (
            scale
            * lax.dot_general(
                photo, text, (((1,), (1,)), ((), ())), preferred_element_type=F32
            )
            + bias
        )
        return (-target * jax.nn.sigmoid(-target * scores)).astype(BF)

    def text_term(w):
        return scale * lax.dot_general(
            w, photo, (((0,), (0,)), ((), ())), preferred_element_type=F32
        )

    w0 = weight(caption, own_target)
    going, w0 = lax.optimization_barrier((caption, w0))
    text2 = sent(going, 2)
    w1 = weight(text1, F32(-1.0))
    term1 = text_term(w1).astype(BF)
    early = jnp.dot(w0, caption, preferred_element_type=F32) + jnp.dot(
        w1, text1, preferred_element_type=F32
    )
    text2, term1, early = lax.optimization_barrier((text2, term1, early))
    w2 = weight(text2, F32(-1.0))

    def image_part(rows):
        return scale * (
            early[rows] + jnp.dot(w2[rows], text2, preferred_element_type=F32)
        )

    give = image_part(slice(0, 2 * width)).astype(BF)
    give, w2, term1 = lax.optimization_barrier((give, w2, term1))
    got = swapped(give, 1)
    keep = image_part(slice(2 * width, 4 * width))
    far = (keep[:width] + got[:width].astype(F32)).astype(BF)
    near = keep[width:] + got[width:].astype(F32)
    term2 = text_term(w2).astype(BF)
    back2 = turned(term2, 2)
    w0, term1, term2 = lax.optimization_barrier((w0, term1, term2))
    back1 = lax.ppermute(term1, AXES, [(j, i) for i, j in route(1)])
    text_grad = text_term(w0)
    other = swapped(far, 2)
    x = lax.axis_index("blk") % X
    down = handed_down(back2)
    own2 = jnp.where(x >= X - 2, F32(0.0), back2.astype(F32))

    image_grad = near + other.astype(F32)
    image_grad, down = lax.optimization_barrier((image_grad, down))
    text_grad = text_grad + back1.astype(F32) + own2 + down.astype(F32)
    return image_grad, text_grad


def solution(mesh):
    in_specs = (P("blk", None), P(("blk", "grp"), None), P("blk", None), P(), P())
    out_specs = (P(("blk", "grp"), None), P(("blk", "grp"), None))
    return jax.shard_map(
        on_device, mesh=mesh, in_specs=in_specs, out_specs=out_specs, check_vma=False
    )
```

```python
import jax
import jax.numpy as jnp
from jax import lax
from jax.sharding import PartitionSpec as P

BF = jnp.bfloat16
F32 = jnp.float32
AXES = ("blk", "grp")
X, Y = 4, 4


def route(distance):
    blocks, parts = lax.axis_size("blk"), lax.axis_size("grp")
    pairs = []
    for b in range(blocks):
        to = (b + distance) % blocks
        wraps = (b // X) % Y > (to // X) % Y
        for g in range(parts):
            pairs.append((b * parts + g, to * parts + (g ^ 2 if wraps else g)))
    return pairs


def sent(block, distance):
    return lax.ppermute(block, AXES, route(distance))


def turned(block, distance):
    blocks = lax.axis_size("blk")
    return lax.ppermute(
        block,
        "blk",
        [(b, b // X * X + (b - distance) % X) for b in range(blocks)],
    )


def handed_down(block):
    parts = lax.axis_size("grp")
    crossing = [(i, j) for i, j in route(X) if i // parts % X >= X - 2]
    return lax.ppermute(block, AXES, [(j, i) for i, j in crossing])


def swapped(block, bit):
    n = lax.axis_size("grp")
    return lax.ppermute(block, "grp", [(i, i ^ bit) for i in range(n)])


def on_device(photo, caption, matching_column, scale_exponent, score_intercept):
    scale = jnp.exp(scale_exponent[0])
    bias = score_intercept[0]
    width = caption.shape[0]
    place = lax.axis_index("grp")

    text1 = sent(caption, 1)

    def ordered(rows):
        parts = [
            lax.dynamic_slice_in_dim(rows, (place ^ bits) * width, width, 0)
            for bits in (3, 1, 2, 0)
        ]
        return jnp.concatenate(parts, 0)

    photo = ordered(photo)
    columns = place * width + lax.iota(jnp.int32, width)
    matched = ordered(matching_column[0])[:, None] == columns[None, :]
    own_target = jnp.where(matched, F32(1.0), F32(-1.0))

    def weight(text, target):
        scores = (
            scale
            * lax.dot_general(
                photo, text, (((1,), (1,)), ((), ())), preferred_element_type=F32
            )
            + bias
        )
        return (-target * jax.nn.sigmoid(-target * scores)).astype(BF)

    def text_term(w):
        return scale * lax.dot_general(
            w, photo, (((0,), (0,)), ((), ())), preferred_element_type=F32
        )

    w0 = weight(caption, own_target)
    going, w0 = lax.optimization_barrier((caption, w0))
    text2 = sent(going, 2)
    w1 = weight(text1, F32(-1.0))
    term1 = text_term(w1).astype(BF)

    def product(w, rows, text):
        return jnp.dot(w[rows], text, preferred_element_type=F32)

    theirs, ours = slice(0, 2 * width), slice(2 * width, 4 * width)
    early = product(w0, theirs, caption) + product(w1, theirs, text1)
    text2, term1, early = lax.optimization_barrier((text2, term1, early))
    w2 = weight(text2, F32(-1.0))
    give = (scale * (early + product(w2, theirs, text2))).astype(BF)
    give, w0, w1, w2, term1 = lax.optimization_barrier((give, w0, w1, w2, term1))
    got = swapped(give, 1)
    keep = product(w0, ours, caption) + product(w1, ours, text1)
    keep, w2 = lax.optimization_barrier((keep, w2))
    keep = scale * (keep + product(w2, ours, text2))
    far = (keep[:width] + got[:width].astype(F32)).astype(BF)
    near = keep[width:] + got[width:].astype(F32)
    term2 = text_term(w2).astype(BF)
    back2 = turned(term2, 2)
    w0, term1, _ = lax.optimization_barrier((w0, term1, term2))
    back1 = lax.ppermute(term1, AXES, [(j, i) for i, j in route(1)])
    other = swapped(far, 2)
    text_grad = text_term(w0)
    x = lax.axis_index("blk") % X
    down = handed_down(back2)
    own2 = jnp.where(x >= X - 2, F32(0.0), back2.astype(F32))

    image_grad = near + other.astype(F32)
    image_grad, down = lax.optimization_barrier((image_grad, down))
    text_grad = text_grad + back1.astype(F32) + own2 + down.astype(F32)
    return image_grad, text_grad


def solution(mesh):
    in_specs = (P("blk", None), P(("blk", "grp"), None), P("blk", None), P(), P())
    out_specs = (P(("blk", "grp"), None), P(("blk", "grp"), None))
    return jax.shard_map(
        on_device, mesh=mesh, in_specs=in_specs, out_specs=out_specs, check_vma=False
    )
```

```python
import jax
import jax.numpy as jnp
from jax import lax
from jax.sharding import PartitionSpec as P

BF = jnp.bfloat16
F32 = jnp.float32
AXES = ("blk", "grp")
X, Y = 4, 4


def route(distance):
    blocks, parts = lax.axis_size("blk"), lax.axis_size("grp")
    pairs = []
    for b in range(blocks):
        to = (b + distance) % blocks
        wraps = (b // X) % Y > (to // X) % Y
        for g in range(parts):
            pairs.append((b * parts + g, to * parts + (g ^ 2 if wraps else g)))
    return pairs


def sent(block, distance):
    return lax.ppermute(block, AXES, route(distance))


def turned(block, distance):
    blocks = lax.axis_size("blk")
    return lax.ppermute(
        block,
        "blk",
        [(b, b // X * X + (b - distance) % X) for b in range(blocks)],
    )


def handed_down(block):
    parts = lax.axis_size("grp")
    crossing = [(i, j) for i, j in route(X) if i // parts % X >= X - 2]
    return lax.ppermute(block, AXES, [(j, i) for i, j in crossing])


def swapped(block, bit):
    n = lax.axis_size("grp")
    return lax.ppermute(block, "grp", [(i, i ^ bit) for i in range(n)])


def on_device(photo, caption, matching_column, scale_exponent, score_intercept):
    scale = jnp.exp(scale_exponent[0])
    bias = score_intercept[0]
    width = caption.shape[0]
    place = lax.axis_index("grp")

    text1 = sent(caption, 1)

    def ordered(rows):
        parts = [
            lax.dynamic_slice_in_dim(rows, (place ^ bits) * width, width, 0)
            for bits in (3, 1, 2, 0)
        ]
        return jnp.concatenate(parts, 0)

    photo = ordered(photo)
    columns = place * width + lax.iota(jnp.int32, width)
    matched = ordered(matching_column[0])[:, None] == columns[None, :]
    own_target = jnp.where(matched, F32(1.0), F32(-1.0))

    def weight(text, target):
        scores = (
            scale
            * lax.dot_general(
                photo, text, (((1,), (1,)), ((), ())), preferred_element_type=F32
            )
            + bias
        )
        return (-target * jax.nn.sigmoid(-target * scores)).astype(BF)

    def text_term(w):
        return scale * lax.dot_general(
            w, photo, (((0,), (0,)), ((), ())), preferred_element_type=F32
        )

    w0 = weight(caption, own_target)
    going, w0 = lax.optimization_barrier((caption, w0))
    text2 = sent(going, 2)
    w1 = weight(text1, F32(-1.0))
    term1 = text_term(w1).astype(BF)

    def product(w, rows, text):
        return jnp.dot(w[rows], text, preferred_element_type=F32)

    theirs, ours = slice(0, 2 * width), slice(2 * width, 4 * width)
    early = product(w0, theirs, caption) + product(w1, theirs, text1)
    text2, term1, early = lax.optimization_barrier((text2, term1, early))
    w2 = weight(text2, F32(-1.0))
    give = (scale * (early + product(w2, theirs, text2))).astype(BF)
    give, w0, w1, w2, term1 = lax.optimization_barrier((give, w0, w1, w2, term1))
    got = swapped(give, 1)
    keep = product(w0, ours, caption) + product(w1, ours, text1)
    keep, w2 = lax.optimization_barrier((keep, w2))
    keep = scale * (keep + product(w2, ours, text2))
    far = (keep[:width] + got[:width].astype(F32)).astype(BF)
    near = keep[width:] + got[width:].astype(F32)
    other = swapped(far, 2)
    w2, _ = lax.optimization_barrier((w2, far))
    term2 = text_term(w2).astype(BF)
    back2 = turned(term2, 2)
    w0, term1, _ = lax.optimization_barrier((w0, term1, term2))
    back1 = lax.ppermute(term1, AXES, [(j, i) for i, j in route(1)])
    text_grad = text_term(w0)

    image_grad = near + other.astype(F32)
    back2, _ = lax.optimization_barrier((back2, image_grad))
    x = lax.axis_index("blk") % X
    down = handed_down(jnp.where(x >= X - 2, back2, BF(0.0)))
    text_grad = text_grad + jnp.where(x >= X - 2, F32(0.0), back2.astype(F32))
    text_grad = text_grad + back1.astype(F32) + down.astype(F32)
    return image_grad, text_grad


def solution(mesh):
    in_specs = (P("blk", None), P(("blk", "grp"), None), P("blk", None), P(), P())
    out_specs = (P(("blk", "grp"), None), P(("blk", "grp"), None))
    return jax.shard_map(
        on_device, mesh=mesh, in_specs=in_specs, out_specs=out_specs, check_vma=False
    )
```

```python
import jax
import jax.numpy as jnp
from jax import lax
from jax.sharding import PartitionSpec as P

BF = jnp.bfloat16
F32 = jnp.float32
AXES = ("blk", "grp")
X, Y = 4, 4


def route(distance):
    blocks, parts = lax.axis_size("blk"), lax.axis_size("grp")
    pairs = []
    for b in range(blocks):
        to = (b + distance) % blocks
        wraps = (b // X) % Y > (to // X) % Y
        for g in range(parts):
            pairs.append((b * parts + g, to * parts + (g ^ 2 if wraps else g)))
    return pairs


def sent(block, distance):
    return lax.ppermute(block, AXES, route(distance))


def turned(block, distance):
    blocks = lax.axis_size("blk")
    return lax.ppermute(
        block,
        "blk",
        [(b, b // X * X + (b - distance) % X) for b in range(blocks)],
    )


def handed_down(block):
    parts = lax.axis_size("grp")
    crossing = [(i, j) for i, j in route(X) if i // parts % X >= X - 2]
    return lax.ppermute(block, AXES, [(j, i) for i, j in crossing])


def swapped(block, bit):
    n = lax.axis_size("grp")
    return lax.ppermute(block, "grp", [(i, i ^ bit) for i in range(n)])


def on_device(photo, caption, matching_column, scale_exponent, score_intercept):
    scale = jnp.exp(scale_exponent[0])
    bias = score_intercept[0]
    width = caption.shape[0]
    place = lax.axis_index("grp")

    text1 = sent(caption, 1)

    def ordered(rows):
        parts = [
            lax.dynamic_slice_in_dim(rows, (place ^ bits) * width, width, 0)
            for bits in (3, 1, 2, 0)
        ]
        return jnp.concatenate(parts, 0)

    photo = ordered(photo)
    columns = place * width + lax.iota(jnp.int32, width)
    matched = ordered(matching_column[0])[:, None] == columns[None, :]
    own_target = jnp.where(matched, F32(1.0), F32(-1.0))

    def weight(text, target):
        scores = (
            scale
            * lax.dot_general(
                photo, text, (((1,), (1,)), ((), ())), preferred_element_type=F32
            )
            + bias
        )
        return (-target * jax.nn.sigmoid(-target * scores)).astype(BF)

    def text_term(w):
        return scale * lax.dot_general(
            w, photo, (((0,), (0,)), ((), ())), preferred_element_type=F32
        )

    w0 = weight(caption, own_target)
    going, w0 = lax.optimization_barrier((caption, w0))
    text2 = sent(going, 2)
    w1 = weight(text1, F32(-1.0))
    term1 = text_term(w1).astype(BF)

    def product(w, rows, text):
        return jnp.dot(w[rows], text, preferred_element_type=F32)

    theirs, ours = slice(0, 2 * width), slice(2 * width, 4 * width)
    early = product(w0, theirs, caption) + product(w1, theirs, text1)
    text2, term1, early = lax.optimization_barrier((text2, term1, early))
    w2 = weight(text2, F32(-1.0))
    give = (scale * (early + product(w2, theirs, text2))).astype(BF)
    give, w0, w1, w2, term1 = lax.optimization_barrier((give, w0, w1, w2, term1))
    got = swapped(give, 1)
    keep = scale * (
        product(w0, ours, caption) + product(w1, ours, text1) + product(w2, ours, text2)
    )
    w2, _ = lax.optimization_barrier((w2, keep))
    far = (keep[:width] + got[:width].astype(F32)).astype(BF)
    near = keep[width:] + got[width:].astype(F32)
    term2 = text_term(w2).astype(BF)
    back2 = turned(term2, 2)
    w0, term1, _ = lax.optimization_barrier((w0, term1, term2))
    back1 = lax.ppermute(term1, AXES, [(j, i) for i, j in route(1)])
    other = swapped(far, 2)
    w0, _ = lax.optimization_barrier((w0, far))
    text_grad = text_term(w0)
    x = lax.axis_index("blk") % X
    down = handed_down(jnp.where(x >= X - 2, back2, BF(0.0)))
    own2 = jnp.where(x >= X - 2, F32(0.0), back2.astype(F32))

    image_grad = near + other.astype(F32)
    image_grad, down = lax.optimization_barrier((image_grad, down))
    text_grad = text_grad + back1.astype(F32) + own2 + down.astype(F32)
    return image_grad, text_grad


def solution(mesh):
    in_specs = (P("blk", None), P(("blk", "grp"), None), P("blk", None), P(), P())
    out_specs = (P(("blk", "grp"), None), P(("blk", "grp"), None))
    return jax.shard_map(
        on_device, mesh=mesh, in_specs=in_specs, out_specs=out_specs, check_vma=False
    )
```

```python
import jax
import jax.numpy as jnp
from jax import lax
from jax.sharding import PartitionSpec as P

BF = jnp.bfloat16
F32 = jnp.float32
AXES = ("blk", "grp")
X, Y = 4, 4


def route(distance):
    blocks, parts = lax.axis_size("blk"), lax.axis_size("grp")
    pairs = []
    for b in range(blocks):
        to = (b + distance) % blocks
        wraps = (b // X) % Y > (to // X) % Y
        for g in range(parts):
            pairs.append((b * parts + g, to * parts + (g ^ 2 if wraps else g)))
    return pairs


def sent(block, distance):
    return lax.ppermute(block, AXES, route(distance))


def turned(block, distance):
    blocks = lax.axis_size("blk")
    return lax.ppermute(
        block,
        "blk",
        [(b, b // X * X + (b - distance) % X) for b in range(blocks)],
    )


def handed_down(block):
    parts = lax.axis_size("grp")
    crossing = [(i, j) for i, j in route(X) if i // parts % X >= X - 2]
    return lax.ppermute(block, AXES, [(j, i) for i, j in crossing])


def swapped(block, bit):
    n = lax.axis_size("grp")
    return lax.ppermute(block, "grp", [(i, i ^ bit) for i in range(n)])


def on_device(photo, caption, matching_column, scale_exponent, score_intercept):
    scale = jnp.exp(scale_exponent[0])
    bias = score_intercept[0]
    width = caption.shape[0]
    place = lax.axis_index("grp")

    text1 = sent(caption, 1)

    def ordered(rows):
        parts = [
            lax.dynamic_slice_in_dim(rows, (place ^ bits) * width, width, 0)
            for bits in (3, 1, 2, 0)
        ]
        return jnp.concatenate(parts, 0)

    photo = ordered(photo)
    columns = place * width + lax.iota(jnp.int32, width)
    matched = ordered(matching_column[0])[:, None] == columns[None, :]
    own_target = jnp.where(matched, F32(1.0), F32(-1.0))

    def weight(text, target):
        scores = (
            scale
            * lax.dot_general(
                photo, text, (((1,), (1,)), ((), ())), preferred_element_type=F32
            )
            + bias
        )
        return (-target * jax.nn.sigmoid(-target * scores)).astype(BF)

    def text_term(w):
        return scale * lax.dot_general(
            w, photo, (((0,), (0,)), ((), ())), preferred_element_type=F32
        )

    w0 = weight(caption, own_target)
    going, w0 = lax.optimization_barrier((caption, w0))
    text2 = sent(going, 2)
    w1 = weight(text1, F32(-1.0))
    term1 = text_term(w1).astype(BF)

    def product(w, rows, text):
        return jnp.dot(w[rows], text, preferred_element_type=F32)

    theirs, ours = slice(0, 2 * width), slice(2 * width, 4 * width)
    early = product(w0, theirs, caption) + product(w1, theirs, text1)
    text2, term1, early = lax.optimization_barrier((text2, term1, early))
    w2 = weight(text2, F32(-1.0))
    give = (scale * (early + product(w2, theirs, text2))).astype(BF)
    give, w0, w1, w2, term1 = lax.optimization_barrier((give, w0, w1, w2, term1))
    got = swapped(give, 1)
    keep = scale * (
        product(w0, ours, caption) + product(w1, ours, text1) + product(w2, ours, text2)
    )
    w2, _ = lax.optimization_barrier((w2, keep))
    far = (keep[:width] + got[:width].astype(F32)).astype(BF)
    near = keep[width:] + got[width:].astype(F32)
    term2 = text_term(w2).astype(BF)
    back2 = turned(term2, 2)
    other = swapped(far, 2)
    w0, _ = lax.optimization_barrier((w0, far))
    text_grad = text_term(w0)
    x = lax.axis_index("blk") % X
    going = jnp.where(x >= X - 2, back2, BF(0.0))
    down = handed_down(going)
    term1, _ = lax.optimization_barrier((term1, going))
    back1 = lax.ppermute(term1, AXES, [(j, i) for i, j in route(1)])
    own2 = jnp.where(x >= X - 2, F32(0.0), back2.astype(F32))

    image_grad = near + other.astype(F32)
    image_grad, down = lax.optimization_barrier((image_grad, down))
    text_grad = text_grad + back1.astype(F32) + own2 + down.astype(F32)
    return image_grad, text_grad


def solution(mesh):
    in_specs = (P("blk", None), P(("blk", "grp"), None), P("blk", None), P(), P())
    out_specs = (P(("blk", "grp"), None), P(("blk", "grp"), None))
    return jax.shard_map(
        on_device, mesh=mesh, in_specs=in_specs, out_specs=out_specs, check_vma=False
    )
```

```python
import jax
import jax.numpy as jnp
from jax import lax
from jax.sharding import PartitionSpec as P

BF = jnp.bfloat16
F32 = jnp.float32
AXES = ("blk", "grp")
X, Y = 4, 4


def route(distance):
    blocks, parts = lax.axis_size("blk"), lax.axis_size("grp")
    pairs = []
    for b in range(blocks):
        to = (b + distance) % blocks
        wraps = (b // X) % Y > (to // X) % Y
        for g in range(parts):
            pairs.append((b * parts + g, to * parts + (g ^ 2 if wraps else g)))
    return pairs


def sent(block, distance):
    return lax.ppermute(block, AXES, route(distance))


def turned(block, distance):
    blocks = lax.axis_size("blk")
    return lax.ppermute(
        block,
        "blk",
        [(b, b // X * X + (b - distance) % X) for b in range(blocks)],
    )


def handed_down(block):
    parts = lax.axis_size("grp")
    crossing = [(i, j) for i, j in route(X) if i // parts % X >= X - 2]
    return lax.ppermute(block, AXES, [(j, i) for i, j in crossing])


def swapped(block, bit):
    n = lax.axis_size("grp")
    return lax.ppermute(block, "grp", [(i, i ^ bit) for i in range(n)])


def on_device(photo, caption, matching_column, scale_exponent, score_intercept):
    scale = jnp.exp(scale_exponent[0])
    bias = score_intercept[0]
    width = caption.shape[0]
    place = lax.axis_index("grp")

    text1 = sent(caption, 1)

    def ordered(rows):
        parts = [
            lax.dynamic_slice_in_dim(rows, (place ^ bits) * width, width, 0)
            for bits in (3, 1, 2, 0)
        ]
        return jnp.concatenate(parts, 0)

    photo = ordered(photo)
    columns = place * width + lax.iota(jnp.int32, width)
    matched = ordered(matching_column[0])[:, None] == columns[None, :]
    own_target = jnp.where(matched, F32(1.0), F32(-1.0))

    def weight(text, target):
        scores = (
            scale
            * lax.dot_general(
                photo, text, (((1,), (1,)), ((), ())), preferred_element_type=F32
            )
            + bias
        )
        return (-target * jax.nn.sigmoid(-target * scores)).astype(BF)

    def text_term(w):
        return scale * lax.dot_general(
            w, photo, (((0,), (0,)), ((), ())), preferred_element_type=F32
        )

    w0 = weight(caption, own_target)
    going, w0 = lax.optimization_barrier((caption, w0))
    text2 = sent(going, 2)
    w1 = weight(text1, F32(-1.0))
    term1 = text_term(w1).astype(BF)

    def product(w, rows, text):
        return jnp.dot(w[rows], text, preferred_element_type=F32)

    theirs, ours = slice(0, 2 * width), slice(2 * width, 4 * width)
    early = product(w0, theirs, caption) + product(w1, theirs, text1)
    text2, term1, early = lax.optimization_barrier((text2, term1, early))
    w2 = weight(text2, F32(-1.0))
    term2 = text_term(w2).astype(BF)
    back2 = turned(term2, 2)
    w2, _ = lax.optimization_barrier((w2, term2))
    give = (scale * (early + product(w2, theirs, text2))).astype(BF)
    give, w0, w1, w2, term1 = lax.optimization_barrier((give, w0, w1, w2, term1))
    got = swapped(give, 1)
    keep = scale * (
        product(w0, ours, caption) + product(w1, ours, text1) + product(w2, ours, text2)
    )
    far = (keep[:width] + got[:width].astype(F32)).astype(BF)
    near = keep[width:] + got[width:].astype(F32)
    other = swapped(far, 2)
    w0, _ = lax.optimization_barrier((w0, far))
    text_grad = text_term(w0)
    x = lax.axis_index("blk") % X
    going = jnp.where(x >= X - 2, back2, BF(0.0))
    down = handed_down(going)
    term1, _ = lax.optimization_barrier((term1, going))
    back1 = lax.ppermute(term1, AXES, [(j, i) for i, j in route(1)])
    own2 = jnp.where(x >= X - 2, F32(0.0), back2.astype(F32))

    image_grad = near + other.astype(F32)
    image_grad, down = lax.optimization_barrier((image_grad, down))
    text_grad = text_grad + back1.astype(F32) + own2 + down.astype(F32)
    return image_grad, text_grad


def solution(mesh):
    in_specs = (P("blk", None), P(("blk", "grp"), None), P("blk", None), P(), P())
    out_specs = (P(("blk", "grp"), None), P(("blk", "grp"), None))
    return jax.shard_map(
        on_device, mesh=mesh, in_specs=in_specs, out_specs=out_specs, check_vma=False
    )
```
